512 devices in a mesh: band: 16 (over z_hi, y), fft: 32 (over x, z_lo, core).
Axes of the slice: x: 4, y: 4, z: 16 (z_hi: 4, z_lo: 4; z = z_hi * 4 + z_lo), core: 2. Of those that a mesh axis runs over, the one named last changes fastest.
Arguments:
- orbitals: bfloat16 [64, 128, 128, 128], P('band', 'fft'), may hold values from -6 to 6
- kernel: float32 [128, 128, 128], P(None, 'fft'), may hold values from 0.05 to 2, as said below
- pairing: int32 [16, 4], P('band'), may hold values from 0 to 3, each once within a row
- owner: int32 [1], replicated, may hold values from 0 to 65535
Outputs:
- exchange: float32 [64, 128, 128, 128], P('band', 'fft')
The draws below stay inside these ranges and needn't reach their ends.
Inputs may be any that keep to these rules, and one draw needn't show every extreme that they name: Each row of pairing is a permutation of 0 to 3. kernel is symmetric under k -> -k: kernel[kz, ky, kx] = kernel[(-kz) mod 128, (-ky) mod 128, (-kx) mod 128].
All inputs are finite; a program needn't handle non-finite values.
Results may differ from the reference program's by a relative error of at most 0.0005.
Values may be sent and summed in bfloat16 or wider, within the bound.
A program may use at most 64 MiB of HBM per device.

```python
import jax
import jax.numpy as jnp
from jax import lax

N = 128
BAND_DEV = 4
BANDS = 64
N_BAND = 16


def draw_kernel(key, part):
    key = jax.random.fold_in(key, 11)
    low = jnp.log(jnp.float32(0.05))
    high = jnp.log(jnp.float32(2.0))
    values = jnp.exp(jax.random.uniform(key, (N, N, N), jnp.float32, low, high))
    mirrored = jnp.roll(jnp.flip(values, (0, 1, 2)), 1, axis=(0, 1, 2))
    return (0.5 * (values + mirrored)).astype(jnp.float32)


def level_of(key, extent, cuts, least, largest):
    gain = 1.0
    for axis_at, parts in cuts:
        steps = jax.random.uniform(jax.random.fold_in(jax.random.fold_in(key, 6), axis_at), (parts,), jnp.float32, least / len(cuts), largest / len(cuts))
        gain = gain * jnp.repeat(jnp.exp(steps), extent[axis_at] // parts).reshape((-1,) + (1,) * (len(extent) - 1 - axis_at))
    return gain


def scatter_about(stream_key, extent, width, most, pieces=(), held_as=jnp.bfloat16):
    array = jax.random.normal(stream_key, extent, jnp.float32) * width
    if len(pieces) > 0:
        array = level_of(stream_key, extent, pieces, -0.22, 0.18) * array
    return jnp.clip(array, min=-most, max=most).astype(held_as)


def setup_inputs(seed: int = 0) -> dict:
    streams_of = jax.random.split(jax.random.key(seed), 5)
    return {
        "orbitals": scatter_about(streams_of[0], (BANDS, N, N, N), 1.0, 6.0, ((0, 16), (1, 32))),
        "kernel": draw_kernel(jax.random.fold_in(streams_of[4], 71), 0),
        "pairing": jax.vmap(lambda own: jax.random.permutation(own, BAND_DEV))(jax.random.split(streams_of[2], N_BAND)).reshape((N_BAND, BAND_DEV)).astype(jnp.int32),
        "owner": jax.random.randint(streams_of[3], (1,), 0, 4096 * N_BAND).astype(jnp.int32),
    }


def reference(orbitals, kernel, pairing, owner):
    group = (owner[0] % N_BAND).astype(jnp.int32)
    first_row = (group * BAND_DEV).astype(jnp.int32)
    orbital_block = lax.dynamic_slice_in_dim(orbitals, first_row, BAND_DEV, 0)
    flat_pairs = pairing.reshape(-1)

    def pair_term(band_index):
        own_band = orbitals[band_index].astype(jnp.float32)
        partner = orbital_block[flat_pairs[band_index]].astype(jnp.float32)
        density = partner * own_band
        field = jnp.fft.ifftn(kernel * jnp.fft.fftn(density))
        return -(partner * jnp.real(field))

    return lax.map(pair_term, jnp.arange(BANDS, dtype=jnp.int32))
```

```python
import functools

import jax
import jax.numpy as jnp
import ml_dtypes
import numpy as np
from jax import lax
from jax.experimental import pallas as pl
from jax.experimental.pallas import tpu as pltpu
from jax.sharding import PartitionSpec as P

MESH = pl.DeviceIdType.MESH
N = 128
FFT = 32
TOP = 32767.0


def halves(table):
    high = table.astype(ml_dtypes.bfloat16)
    low = (table - high.astype(np.float64)).astype(ml_dtypes.bfloat16)
    return high, low


def tables():
    counter = np.arange(N)
    phase = (np.outer(counter, counter) % N) * (2.0 * np.pi / N)
    cosine, sine = np.cos(phase), np.sin(phase)
    forward = np.block([[cosine, sine], [-sine, cosine]])
    inverse = np.block([[cosine, -sine], [sine, cosine]]) / N
    to_columns = forward.reshape(2, FFT, 4, 2 * N).transpose(1, 0, 2, 3).reshape(2 * N, 2 * N)
    to_planes = inverse.reshape(2, FFT, 4, 2 * N).transpose(1, 2, 0, 3).reshape(2 * N, 2 * N)

    def left(table):
        high, low = halves(table)
        return np.concatenate([high, high, low], axis=1)

    def right(table):
        high, low = halves(table.T)
        return np.concatenate([high, high, low], axis=0)

    lefts = np.stack([left(to_columns), left(forward), left(to_planes), left(inverse)])
    rights = np.stack([right(forward), right(inverse)])
    return lefts, rights


def split(value):
    high = value.astype(jnp.bfloat16)
    low = (value - high.astype(jnp.float32)).astype(jnp.bfloat16)
    return high, low


def dot(a, b):
    return jnp.dot(a, b, preferred_element_type=jnp.float32)


def code(value, inverse_scale):
    ratio = value * inverse_scale
    root = ratio * lax.rsqrt(jnp.maximum(jnp.abs(ratio), 1e-30))
    return jnp.round(root * TOP).astype(jnp.int32).astype(jnp.int16)


def exchange_kernel(
    root_z,
    owner_ref, pair_ref, own_hbm, kernel_hbm, left_hbm, right_hbm,
    out_ref,
    own, table_l, table_r, weight, cand, block,
    send, recv, scale_out, scale_in,
    decoded, rhs, mid, product,
    load_sem, cand_send, cand_recv, ring_send, ring_recv, mate_send, mate_recv,
    data_send, data_recv, scale_send, scale_recv, own_sem,
):
    me = lax.axis_index("fft")
    group = lax.axis_index("band")
    y, z = lax.rem(group, 4), group // 4
    right_z, left_z = lax.rem(z + 1, 4) * 4 + y, lax.rem(z + 3, 4) * 4 + y

    loads = [
        pltpu.make_async_copy(own_hbm, own, load_sem.at[0]),
        pltpu.make_async_copy(left_hbm, table_l, load_sem.at[1]),
        pltpu.make_async_copy(right_hbm, table_r, load_sem.at[2]),
        pltpu.make_async_copy(kernel_hbm, weight, load_sem.at[3]),
    ]
    for load in loads:
        load.start()

    barrier = pltpu.get_barrier_semaphore()

    def mate(k):
        return z * 4 + lax.rem(y + k, 4)

    for k in range(1, 4):
        pl.semaphore_signal(barrier, inc=1, device_id={"band": mate(k)}, device_id_type=MESH)
    for other in (right_z, left_z):
        pl.semaphore_signal(barrier, inc=1, device_id={"band": other}, device_id_type=MESH)

    def greet(i, carry):
        pl.semaphore_signal(
            barrier, inc=1, device_id={"fft": lax.rem(me + i, FFT)}, device_id_type=MESH
        )
        return carry

    lax.fori_loop(1, FFT, greet, 0)
    pl.semaphore_wait(barrier, 5 + FFT - 1)

    def rows(half):
        return pl.ds(half * (N // 2), N // 2)

    def pass_on(p, half):
        there = right_z if half == 0 else left_z
        pltpu.make_async_remote_copy(
            block.at[p, y, rows(half)], block.at[p, y, rows(half)],
            ring_send, ring_recv.at[p, half],
            device_id={"band": there}, device_id_type=MESH,
        ).start()

    def arrived(p, half):
        here = block.at[p, y, rows(half)]
        pltpu.make_async_copy(here, here, ring_recv.at[p, half]).wait()

    def share(p, half):
        for k in range(1, 4):
            pltpu.make_async_remote_copy(
                block.at[p, y, rows(half)], block.at[p, y, rows(half)],
                mate_send, mate_recv.at[p],
                device_id={"band": mate(k)}, device_id_type=MESH,
            ).start()

    place = lax.rem(z - root_z + 4, 4)

    @pl.when(place == 0)
    def _():
        for p in range(4):
            for k in range(1, 4):
                there = lax.rem(y + k, 4)
                pltpu.make_async_remote_copy(
                    own_hbm.at[p, there], cand.at[p, y],
                    cand_send, cand_recv.at[p],
                    device_id={"band": mate(k)}, device_id_type=MESH,
                ).start()
        loads[0].wait()
        root_y = lax.rem(owner_ref[0], 4)
        for p in range(4):
            cand[p, y] = own[p, y]
            pltpu.make_async_copy(
                cand.at[p, pl.ds(0, 3)], cand.at[p, pl.ds(0, 3)], cand_recv.at[p]
            ).wait()
            chosen = cand[p, 0]
            for k in range(1, 4):
                chosen = jnp.where(root_y == k, cand[p, k], chosen)
            block[p, y] = chosen
            pass_on(p, 0)
            pass_on(p, 1)
            share(p, 0)
            share(p, 1)
        pltpu.make_async_copy(cand.at[:, pl.ds(0, 3)], cand.at[:, pl.ds(0, 3)], cand_send).wait()

    @pl.when(place == 1)
    def _():
        for p in range(4):
            arrived(p, 0)
            pass_on(p, 0)
            share(p, 0)
        for p in range(4):
            arrived(p, 1)
            share(p, 1)
        loads[0].wait()

    @pl.when(place == 2)
    def _():
        for p in range(4):
            for half in range(2):
                arrived(p, half)
                pass_on(p, half)
                share(p, half)
        loads[0].wait()

    @pl.when(place == 3)
    def _():
        for p in range(4):
            arrived(p, 1)
            pass_on(p, 1)
            share(p, 1)
        for p in range(4):
            arrived(p, 0)
            share(p, 0)
        loads[0].wait()

    for load in loads[1:]:
        load.wait()

    def own_band(p):
        band = jnp.int32(0)
        for j in range(1, 4):
            band = jnp.where(pair_ref[0, j] == p, j, band)
        return band

    def ship(step, f):
        pltpu.make_async_copy(
            send.at[step, f, me], recv.at[step, f, me], own_sem.at[step, f]
        ).start()

        def one(i, carry):
            there = lax.rem(me + i, FFT)
            pltpu.make_async_remote_copy(
                send.at[step, f, there], recv.at[step, f, me],
                data_send.at[step, f], data_recv.at[step, f],
                device_id={"fft": there}, device_id_type=MESH,
            ).start()
            pltpu.make_async_remote_copy(
                scale_out.at[step, f], scale_in.at[step, f, me],
                scale_send.at[step, f], scale_recv.at[step, f],
                device_id={"fft": there}, device_id_type=MESH,
            ).start()
            return carry

        lax.fori_loop(1, FFT, one, 0)

    def landed(step, f):
        most = pl.ds(0, FFT - 1)
        for buffer, sem in ((recv, data_recv), (scale_in, scale_recv)):
            here = buffer.at[step, f, most]
            pltpu.make_async_copy(here, here, sem.at[step, f]).wait()
        here = recv.at[step, f, 0]
        pltpu.make_async_copy(here, here, own_sem.at[step, f]).wait()

    def encode(step, f, pieces):
        top = jnp.max(jnp.abs(pieces[0]), axis=0, keepdims=True)
        for piece in pieces[1:]:
            top = jnp.maximum(top, jnp.max(jnp.abs(piece), axis=0, keepdims=True))
        top = jnp.maximum(jnp.max(top, axis=1, keepdims=True), 1e-36)
        inverse_scale = 1.0 / top
        scale = jnp.broadcast_to(top * (1.0 / (TOP * TOP)), (1, N))
        scale_out[step, f] = scale
        scale_in[step, f, me] = scale
        for pair in range(2):
            both = jnp.concatenate(
                [pieces[2 * pair].reshape(FFT, 8, N), pieces[2 * pair + 1].reshape(FFT, 8, N)],
                axis=1,
            )
            send[step, f, :, pair] = code(both, inverse_scale)

    def decode(step, f):
        raw = recv[step, f].astype(jnp.int32).astype(jnp.float32)
        value = raw * jnp.abs(raw) * scale_in[step, f].reshape(FFT, 1, 1, N)
        decoded[...] = value.reshape(FFT * 32, N)

    def line(row):
        return decoded[pl.ds(row, N, stride=8), :]

    def put(row, column, value):
        high, low = split(value)
        at = pl.ds(column, value.shape[1])
        rhs[pl.ds(row, N), at] = high
        rhs[pl.ds(row + 2 * N, N), at] = low
        rhs[pl.ds(row + 4 * N, N), at] = high

    def forward(f):
        for p in (2 * f, 2 * f + 1):
            others = block.at[p, pl.ds(0, 3)]
            pltpu.make_async_copy(others, others, mate_recv.at[p]).wait()
        densities = []
        for p in (2 * f, 2 * f + 1):
            density = block[p].astype(jnp.float32) * own[own_band(p)].astype(jnp.float32)
            densities.append(split(density.reshape(4 * N, N)))
        (high_0, low_0), (high_1, low_1) = densities
        lhs = jnp.concatenate([high_0, high_1, low_0, low_1, high_0, high_1], axis=1)
        mid[...] = dot(lhs, table_r[0])
        pieces = []
        for pair in range(2):
            for second in range(2):
                for part in range(2):
                    at = pl.ds((2 * pair + second) * N, N)
                    put(part * N, second * N, mid[at, pl.ds(part * N, N)])
            result = dot(table_l[0], rhs[:, pl.ds(0, 2 * N)])
            pieces += [result[:, :N], result[:, N:]]
        encode(0, f, pieces)
        ship(0, f)

    def middle(f):
        landed(0, f)
        decode(0, f)
        for part in range(2):
            for r in range(4):
                put(part * N, r * N, line(part * 4 + r))
        spectrum = dot(table_l[1], rhs[...])
        for r in range(4):
            factor = weight[pl.ds(r, N, stride=4), :]
            for part in range(2):
                put(part * N, r * N, spectrum[part * N : (part + 1) * N, r * N : (r + 1) * N] * factor)
        result = dot(table_l[2], rhs[...])
        encode(1, f, [result[:, r * N : (r + 1) * N] for r in range(4)])
        ship(1, f)

    def backward(f):
        landed(1, f)
        decode(1, f)
        for pair in range(2):
            for second in range(2):
                for part in range(2):
                    put(part * N, second * N, line((2 * pair + second) * 2 + part))
            field = dot(table_l[3], rhs[:, pl.ds(0, 2 * N)])
            lhs = []
            for second in range(2):
                at = slice(second * N, (second + 1) * N)
                high_0, low_0 = split(field[:N, at])
                high_1, low_1 = split(field[N:, at])
                lhs.append(jnp.concatenate([high_0, high_1, low_0, low_1, high_0, high_1], axis=1))
            potential = dot(jnp.concatenate(lhs, axis=0), table_r[1])
            for part in range(2):
                p = 2 * f + part
                at = pl.ds(2 * pair, 2)
                partner = block[p, at].astype(jnp.float32)
                product[p, at] = -(partner * potential[:, part * N : (part + 1) * N].reshape(2, N, N))

    forward(0)
    forward(1)
    middle(0)
    middle(1)
    backward(0)
    backward(1)

    for j in range(4):
        out_ref[j] = product[pair_ref[0, j]]

    @pl.when(place == 0)
    def _():
        here = block.at[:, 0]
        pltpu.make_async_copy(here, here, ring_send).wait()

    @pl.when(place == 2)
    def _():
        here = block.at[:, 0]
        pltpu.make_async_copy(here, here, ring_send).wait()

    @pl.when(lax.rem(place, 2) == 1)
    def _():
        here = block.at[:, 0, rows(0)]
        pltpu.make_async_copy(here, here, ring_send).wait()

    here = block.at[:, pl.ds(0, 3)]
    pltpu.make_async_copy(here, here, mate_send).wait()
    for step in range(2):
        for f in range(2):
            here = send.at[step, f, pl.ds(0, FFT - 1)]
            pltpu.make_async_copy(here, here, data_send.at[step, f]).wait()
            here = scale_in.at[step, f, pl.ds(0, FFT - 1)]
            pltpu.make_async_copy(here, here, scale_send.at[step, f]).wait()


def call(root_z, owner, pairing, orbitals, kernel, lefts, rights):
    anywhere = pl.BlockSpec(memory_space=pl.ANY)
    scalars = pl.BlockSpec(memory_space=pltpu.SMEM)
    dma = pltpu.SemaphoreType.DMA
    return pl.pallas_call(
        functools.partial(exchange_kernel, root_z),
        out_shape=jax.ShapeDtypeStruct((4, 4, N, N), jnp.float32),
        in_specs=[scalars, scalars, anywhere, anywhere, anywhere, anywhere],
        out_specs=pl.BlockSpec(memory_space=pltpu.VMEM),
        scratch_shapes=[
            pltpu.VMEM((4, 4, N, N), jnp.bfloat16),
            pltpu.VMEM((4, 2 * N, 6 * N), jnp.bfloat16),
            pltpu.VMEM((2, 6 * N, 2 * N), jnp.bfloat16),
            pltpu.VMEM((4 * N, N), jnp.float32),
            pltpu.VMEM((4, 4, N, N), jnp.bfloat16),
            pltpu.VMEM((4, 4, N, N), jnp.bfloat16),
            pltpu.VMEM((2, 2, FFT, 2, 16, N), jnp.int16),
            pltpu.VMEM((2, 2, FFT, 2, 16, N), jnp.int16),
            pltpu.VMEM((2, 2, 1, N), jnp.float32),
            pltpu.VMEM((2, 2, FFT, 1, N), jnp.float32),
            pltpu.VMEM((FFT * 32, N), jnp.float32),
            pltpu.VMEM((6 * N, 4 * N), jnp.bfloat16),
            pltpu.VMEM((4 * N, 2 * N), jnp.float32),
            pltpu.VMEM((4, 4, N, N), jnp.float32),
            dma((4,)),
            dma,
            dma((4,)),
            dma,
            dma((4, 2)),
            dma,
            dma((4,)),
            dma((2, 2)),
            dma((2, 2)),
            dma((2, 2)),
            dma((2, 2)),
            dma((2, 2)),
        ],
        compiler_params=pltpu.CompilerParams(
            collective_id=root_z, has_side_effects=True, vmem_limit_bytes=48 * 1024 * 1024
        ),
    )(owner, pairing, orbitals, kernel, lefts, rights)


def local(orbitals, kernel, pairing, owner):
    lefts, rights = tables()
    root_z = (owner[0] % 16) // 4
    return lax.switch(
        root_z,
        [functools.partial(call, k) for k in range(4)],
        owner, pairing, orbitals, kernel.reshape(4 * N, N), jnp.asarray(lefts), jnp.asarray(rights),
    )


def solution(mesh):
    placed = (P("band", "fft", None, None), P(None, "fft", None), P("band", None), P())
    return jax.shard_map(
        local, mesh=mesh, in_specs=placed, out_specs=P("band", "fft", None, None), check_vma=False
    )
```

```python
import functools

import jax
import jax.numpy as jnp
import ml_dtypes
import numpy as np
from jax import lax
from jax.experimental import pallas as pl
from jax.experimental.pallas import tpu as pltpu
from jax.sharding import PartitionSpec as P

MESH = pl.DeviceIdType.MESH
N = 128
FFT = 32
TOP = 32767.0
DEPTH = 1
RIGHT, LEFT = 0, 1
STEP = 3


def plan(root):
    ring = ((RIGHT,) * 3, (LEFT,) * 3)
    lines = {
        0: tuple(enumerate(ring)),
        1: ((0, (RIGHT,) * 2), (0, (LEFT,)), (1, (LEFT,) * 3)),
        2: tuple(enumerate(ring)),
        3: ((0, (RIGHT,) * 3), (1, (LEFT,) * 2), (1, (RIGHT,))),
    }[root]
    routes = [[] for _ in range(4)]
    steps = [[0, 0] for _ in range(4)]
    for half, ways in lines:
        at = root
        for step, way in enumerate(ways):
            routes[at].append((half, way))
            at = (at + (1 if way == RIGHT else 3)) % 4
            steps[at][half] = step + 1
    return routes, steps


def halves(table):
    high = table.astype(ml_dtypes.bfloat16)
    low = (table - high.astype(np.float64)).astype(ml_dtypes.bfloat16)
    return high, low


def tables():
    counter = np.arange(N)
    phase = (np.outer(counter, counter) % N) * (2.0 * np.pi / N)
    cosine, sine = np.cos(phase), np.sin(phase)
    forward = np.block([[cosine, sine], [-sine, cosine]])
    inverse = np.block([[cosine, -sine], [sine, cosine]]) / N
    to_columns = forward.reshape(2, FFT, 4, 2 * N).transpose(1, 0, 2, 3).reshape(2 * N, 2 * N)
    to_planes = inverse.reshape(2, FFT, 4, 2 * N).transpose(1, 2, 0, 3).reshape(2 * N, 2 * N)

    def left(table):
        high, low = halves(table)
        return np.concatenate([high, high, low], axis=1)

    def right(table):
        high, low = halves(table.T)
        return np.concatenate([high, high, low], axis=0)

    lefts = np.stack([left(to_columns), left(forward), left(to_planes), left(inverse)])
    rights = np.stack([right(forward), right(inverse)])
    return lefts, rights


def split(value):
    high = value.astype(jnp.bfloat16)
    low = (value - high.astype(jnp.float32)).astype(jnp.bfloat16)
    return high, low


def dot(a, b):
    return jnp.dot(a, b, preferred_element_type=jnp.float32)


def code(value, inverse_scale):
    ratio = value * inverse_scale
    root = ratio * lax.rsqrt(jnp.maximum(jnp.abs(ratio), 1e-30))
    return jnp.round(root * TOP).astype(jnp.int32).astype(jnp.int16)


def exchange_kernel(
    root_z,
    owner_ref, pair_ref, own_hbm, kernel_hbm, left_hbm, right_hbm,
    out_ref,
    own, table_l, table_r, weight, cand, block,
    send, recv, scale_out, scale_in,
    decoded, rhs, mid, product,
    load_sem, cand_send, cand_recv, ring_send, ring_recv, mate_send, mate_recv,
    data_send, data_recv, scale_send, scale_recv, own_sem,
):
    routes, steps = plan(root_z)
    me = lax.axis_index("fft")
    group = lax.axis_index("band")
    y, z = lax.rem(group, 4), group // 4
    right_z, left_z = lax.rem(z + 1, 4) * 4 + y, lax.rem(z + 3, 4) * 4 + y

    loads = [
        pltpu.make_async_copy(own_hbm, own, load_sem.at[0]),
        pltpu.make_async_copy(left_hbm, table_l, load_sem.at[1]),
        pltpu.make_async_copy(right_hbm, table_r, load_sem.at[2]),
        pltpu.make_async_copy(kernel_hbm, weight, load_sem.at[3]),
    ]
    for load in loads:
        load.start()

    barrier = pltpu.get_barrier_semaphore()

    def mate(k):
        return z * 4 + lax.rem(y + k, 4)

    for k in range(1, 4):
        pl.semaphore_signal(barrier, inc=1, device_id={"band": mate(k)}, device_id_type=MESH)
    for other in (right_z, left_z):
        pl.semaphore_signal(barrier, inc=1, device_id={"band": other}, device_id_type=MESH)

    def greet(i, carry):
        pl.semaphore_signal(
            barrier, inc=1, device_id={"fft": lax.rem(me + i, FFT)}, device_id_type=MESH
        )
        return carry

    lax.fori_loop(1, FFT, greet, 0)
    pl.semaphore_wait(barrier, 5 + FFT - 1)

    def rows(half):
        return pl.ds(half * (N // 2), N // 2)

    def piece(p, half):
        return block.at[p, y, rows(half)]

    def pass_on(p, half, way):
        there = right_z if way == RIGHT else left_z
        return pltpu.make_async_remote_copy(
            piece(p, half), piece(p, half),
            ring_send.at[p, half, way], ring_recv.at[p, half],
            device_id={"band": there}, device_id_type=MESH,
        )

    def share(p, half):
        for k in range(1, 4):
            pltpu.make_async_remote_copy(
                piece(p, half), piece(p, half),
                mate_send, mate_recv.at[p],
                device_id={"band": mate(k)}, device_id_type=MESH,
            ).start()

    def spread(p):
        for k in range(1, 4):
            there = lax.rem(y + k, 4)
            pltpu.make_async_remote_copy(
                own_hbm.at[p, there], cand.at[p, y],
                cand_send, cand_recv.at[p],
                device_id={"band": mate(k)}, device_id_type=MESH,
            ).start()

    place = lax.rem(z - root_z + 4, 4)

    @pl.when(place == 0)
    def _():
        eager = root_z == 0
        for p in range(4 if eager else 2):
            spread(p)
        loads[0].wait()
        root_y = lax.rem(owner_ref[0], 4)
        for p in range(4):
            cand[p, y] = own[p, y]
        for p in range(4):
            three = cand.at[p, pl.ds(0, 3)]
            pltpu.make_async_copy(three, three, cand_recv.at[p]).wait()
            if p < 2 and not eager:
                spread(p + 2)
            chosen = cand[p, 0]
            for k in range(1, 4):
                chosen = jnp.where(root_y == k, cand[p, k], chosen)
            block[p, y] = chosen
            for half, way in routes[root_z]:
                if p >= DEPTH:
                    pass_on(p - DEPTH, half, way).wait_send()
                pass_on(p, half, way).start()
            if eager:
                share(p, 0)
                share(p, 1)
        for p in () if eager else range(4):
            share(p, 0)
            share(p, 1)
        three = cand.at[:, pl.ds(0, 3)]
        pltpu.make_async_copy(three, three, cand_send).wait()

    def relay(here):
        order = [(steps[here][half] * STEP + p, p, half) for p in range(4) for half in range(2)]
        for _, p, half in sorted(order):
            pltpu.make_async_copy(piece(p, half), piece(p, half), ring_recv.at[p, half]).wait()
            for which, way in routes[here]:
                if which == half:
                    pass_on(p, half, way).start()
            share(p, half)

    for here in range(4):
        if here != root_z:
            pl.when(z == here)(functools.partial(relay, here))

    @pl.when(place != 0)
    def _():
        loads[0].wait()

    for load in loads[1:]:
        load.wait()

    def own_band(p):
        band = jnp.int32(0)
        for j in range(1, 4):
            band = jnp.where(pair_ref[0, j] == p, j, band)
        return band

    def ship(step, f):
        pltpu.make_async_copy(
            send.at[step, f, me], recv.at[step, f, me], own_sem.at[step, f]
        ).start()

        def one(i, carry):
            there = lax.rem(me + i, FFT)
            pltpu.make_async_remote_copy(
                send.at[step, f, there], recv.at[step, f, me],
                data_send.at[step, f], data_recv.at[step, f],
                device_id={"fft": there}, device_id_type=MESH,
            ).start()
            pltpu.make_async_remote_copy(
                scale_out.at[step, f], scale_in.at[step, f, me],
                scale_send.at[step, f], scale_recv.at[step, f],
                device_id={"fft": there}, device_id_type=MESH,
            ).start()
            return carry

        lax.fori_loop(1, FFT, one, 0)

    def landed(step, f):
        most = pl.ds(0, FFT - 1)
        for buffer, sem in ((recv, data_recv), (scale_in, scale_recv)):
            here = buffer.at[step, f, most]
            pltpu.make_async_copy(here, here, sem.at[step, f]).wait()
        here = recv.at[step, f, 0]
        pltpu.make_async_copy(here, here, own_sem.at[step, f]).wait()

    def encode(step, f, pieces):
        top = jnp.max(jnp.abs(pieces[0]), axis=0, keepdims=True)
        for piece in pieces[1:]:
            top = jnp.maximum(top, jnp.max(jnp.abs(piece), axis=0, keepdims=True))
        top = jnp.maximum(jnp.max(top, axis=1, keepdims=True), 1e-36)
        inverse_scale = 1.0 / top
        scale = jnp.broadcast_to(top * (1.0 / (TOP * TOP)), (1, N))
        scale_out[step, f] = scale
        scale_in[step, f, me] = scale
        for pair in range(2):
            both = jnp.concatenate(
                [pieces[2 * pair].reshape(FFT, 8, N), pieces[2 * pair + 1].reshape(FFT, 8, N)],
                axis=1,
            )
            send[step, f, :, pair] = code(both, inverse_scale)

    def decode(step, f):
        raw = recv[step, f].astype(jnp.int32).astype(jnp.float32)
        value = raw * jnp.abs(raw) * scale_in[step, f].reshape(FFT, 1, 1, N)
        decoded[...] = value.reshape(FFT * 32, N)

    def line(row):
        return decoded[pl.ds(row, N, stride=8), :]

    def put(row, column, value):
        high, low = split(value)
        at = pl.ds(column, value.shape[1])
        rhs[pl.ds(row, N), at] = high
        rhs[pl.ds(row + 2 * N, N), at] = low
        rhs[pl.ds(row + 4 * N, N), at] = high

    def forward(f):
        for p in (2 * f, 2 * f + 1):
            others = block.at[p, pl.ds(0, 3)]
            pltpu.make_async_copy(others, others, mate_recv.at[p]).wait()
        densities = []
        for p in (2 * f, 2 * f + 1):
            density = block[p].astype(jnp.float32) * own[own_band(p)].astype(jnp.float32)
            densities.append(split(density.reshape(4 * N, N)))
        (high_0, low_0), (high_1, low_1) = densities
        lhs = jnp.concatenate([high_0, high_1, low_0, low_1, high_0, high_1], axis=1)
        mid[...] = dot(lhs, table_r[0])
        pieces = []
        for pair in range(2):
            for second in range(2):
                for part in range(2):
                    at = pl.ds((2 * pair + second) * N, N)
                    put(part * N, second * N, mid[at, pl.ds(part * N, N)])
            result = dot(table_l[0], rhs[:, pl.ds(0, 2 * N)])
            pieces += [result[:, :N], result[:, N:]]
        encode(0, f, pieces)
        ship(0, f)

    def middle(f):
        landed(0, f)
        decode(0, f)
        for part in range(2):
            for r in range(4):
                put(part * N, r * N, line(part * 4 + r))
        spectrum = dot(table_l[1], rhs[...])
        for r in range(4):
            factor = weight[pl.ds(r, N, stride=4), :]
            for part in range(2):
                put(part * N, r * N, spectrum[part * N : (part + 1) * N, r * N : (r + 1) * N] * factor)
        result = dot(table_l[2], rhs[...])
        encode(1, f, [result[:, r * N : (r + 1) * N] for r in range(4)])
        ship(1, f)

    def backward(f):
        landed(1, f)
        decode(1, f)
        for pair in range(2):
            for second in range(2):
                for part in range(2):
                    put(part * N, second * N, line((2 * pair + second) * 2 + part))
            field = dot(table_l[3], rhs[:, pl.ds(0, 2 * N)])
            lhs = []
            for second in range(2):
                at = slice(second * N, (second + 1) * N)
                high_0, low_0 = split(field[:N, at])
                high_1, low_1 = split(field[N:, at])
                lhs.append(jnp.concatenate([high_0, high_1, low_0, low_1, high_0, high_1], axis=1))
            potential = dot(jnp.concatenate(lhs, axis=0), table_r[1])
            for part in range(2):
                p = 2 * f + part
                at = pl.ds(2 * pair, 2)
                partner = block[p, at].astype(jnp.float32)
                product[p, at] = -(partner * potential[:, part * N : (part + 1) * N].reshape(2, N, N))

    forward(0)
    forward(1)
    middle(0)
    middle(1)
    backward(0)
    backward(1)

    for j in range(4):
        out_ref[j] = product[pair_ref[0, j]]

    def sent(here):
        for p in range(4 - DEPTH if here == root_z else 0, 4):
            for half, way in routes[here]:
                pass_on(p, half, way).wait_send()

    for here in range(4):
        if routes[here]:
            pl.when(z == here)(functools.partial(sent, here))

    here = block.at[:, pl.ds(0, 3)]
    pltpu.make_async_copy(here, here, mate_send).wait()
    for step in range(2):
        for f in range(2):
            here = send.at[step, f, pl.ds(0, FFT - 1)]
            pltpu.make_async_copy(here, here, data_send.at[step, f]).wait()
            here = scale_in.at[step, f, pl.ds(0, FFT - 1)]
            pltpu.make_async_copy(here, here, scale_send.at[step, f]).wait()


def call(root_z, owner, pairing, orbitals, kernel, lefts, rights):
    anywhere = pl.BlockSpec(memory_space=pl.ANY)
    scalars = pl.BlockSpec(memory_space=pltpu.SMEM)
    dma = pltpu.SemaphoreType.DMA
    return pl.pallas_call(
        functools.partial(exchange_kernel, root_z),
        out_shape=jax.ShapeDtypeStruct((4, 4, N, N), jnp.float32),
        in_specs=[scalars, scalars, anywhere, anywhere, anywhere, anywhere],
        out_specs=pl.BlockSpec(memory_space=pltpu.VMEM),
        scratch_shapes=[
            pltpu.VMEM((4, 4, N, N), jnp.bfloat16),
            pltpu.VMEM((4, 2 * N, 6 * N), jnp.bfloat16),
            pltpu.VMEM((2, 6 * N, 2 * N), jnp.bfloat16),
            pltpu.VMEM((4 * N, N), jnp.float32),
            pltpu.VMEM((4, 4, N, N), jnp.bfloat16),
            pltpu.VMEM((4, 4, N, N), jnp.bfloat16),
            pltpu.VMEM((2, 2, FFT, 2, 16, N), jnp.int16),
            pltpu.VMEM((2, 2, FFT, 2, 16, N), jnp.int16),
            pltpu.VMEM((2, 2, 1, N), jnp.float32),
            pltpu.VMEM((2, 2, FFT, 1, N), jnp.float32),
            pltpu.VMEM((FFT * 32, N), jnp.float32),
            pltpu.VMEM((6 * N, 4 * N), jnp.bfloat16),
            pltpu.VMEM((4 * N, 2 * N), jnp.float32),
            pltpu.VMEM((4, 4, N, N), jnp.float32),
            dma((4,)),
            dma,
            dma((4,)),
            dma((4, 2, 2)),
            dma((4, 2)),
            dma,
            dma((4,)),
            dma((2, 2)),
            dma((2, 2)),
            dma((2, 2)),
            dma((2, 2)),
            dma((2, 2)),
        ],
        compiler_params=pltpu.CompilerParams(
            collective_id=root_z, has_side_effects=True, vmem_limit_bytes=48 * 1024 * 1024
        ),
    )(owner, pairing, orbitals, kernel, lefts, rights)


def local(orbitals, kernel, pairing, owner):
    lefts, rights = tables()
    root_z = (owner[0] % 16) // 4
    return lax.switch(
        root_z,
        [functools.partial(call, k) for k in range(4)],
        owner, pairing, orbitals, kernel.reshape(4 * N, N), jnp.asarray(lefts), jnp.asarray(rights),
    )


def solution(mesh):
    placed = (P("band", "fft", None, None), P(None, "fft", None), P("band", None), P())
    return jax.shard_map(
        local, mesh=mesh, in_specs=placed, out_specs=P("band", "fft", None, None), check_vma=False
    )
```

```python
import functools

import jax
import jax.numpy as jnp
import ml_dtypes
import numpy as np
from jax import lax
from jax.experimental import pallas as pl
from jax.experimental.pallas import tpu as pltpu
from jax.sharding import PartitionSpec as P

MESH = pl.DeviceIdType.MESH
N = 128
FFT = 32
TOP = 32767.0
DEPTH = 1
RIGHT, LEFT = 0, 1
STEP = 3


def plan(root):
    ring = ((RIGHT,) * 3, (LEFT,) * 3)
    lines = {
        0: tuple(enumerate(ring)),
        1: ((0, (RIGHT,) * 2), (0, (LEFT,)), (1, (LEFT,) * 3)),
        2: tuple(enumerate(ring)),
        3: ((0, (RIGHT,) * 3), (1, (LEFT,) * 2), (1, (RIGHT,))),
    }[root]
    routes = [[] for _ in range(4)]
    steps = [[0, 0] for _ in range(4)]
    for half, ways in lines:
        at = root
        for step, way in enumerate(ways):
            routes[at].append((half, way))
            at = (at + (1 if way == RIGHT else 3)) % 4
            steps[at][half] = step + 1
    return routes, steps


def halves(table):
    high = table.astype(ml_dtypes.bfloat16)
    low = (table - high.astype(np.float64)).astype(ml_dtypes.bfloat16)
    return high, low


def tables():
    counter = np.arange(N)
    phase = (np.outer(counter, counter) % N) * (2.0 * np.pi / N)
    cosine, sine = np.cos(phase), np.sin(phase)
    forward = np.block([[cosine, sine], [-sine, cosine]])
    inverse = np.block([[cosine, -sine], [sine, cosine]]) / N
    to_columns = forward.reshape(2, FFT, 4, 2 * N).transpose(1, 0, 2, 3).reshape(2 * N, 2 * N)
    to_planes = inverse.reshape(2, FFT, 4, 2 * N).transpose(1, 2, 0, 3).reshape(2 * N, 2 * N)

    def left(table):
        high, low = halves(table)
        return np.concatenate([high, high, low], axis=1)

    def right(table):
        high, low = halves(table.T)
        return np.concatenate([high, high, low], axis=0)

    lefts = np.stack([left(to_columns), left(forward), left(to_planes), left(inverse)])
    rights = np.stack([right(forward), right(inverse)])
    return lefts, rights


def split(value):
    high = value.astype(jnp.bfloat16)
    low = (value - high.astype(jnp.float32)).astype(jnp.bfloat16)
    return high, low


def dot(a, b):
    return jnp.dot(a, b, preferred_element_type=jnp.float32)


def code(value, inverse_scale):
    ratio = value * inverse_scale
    root = ratio * lax.rsqrt(jnp.maximum(jnp.abs(ratio), 1e-30))
    return jnp.round(root * TOP).astype(jnp.int32).astype(jnp.int16)


def exchange_kernel(
    root_z,
    owner_ref, pair_ref, own_hbm, kernel_hbm, left_hbm, right_hbm,
    out_ref,
    own, table_l, table_r, weight, cand, block,
    send, recv, scale_out, scale_in,
    decoded, rhs, mid, product,
    load_sem, cand_send, cand_recv, ring_send, ring_recv, mate_send, mate_recv,
    data_send, data_recv, scale_send, scale_recv, own_sem,
):
    routes, steps = plan(root_z)
    me = lax.axis_index("fft")
    group = lax.axis_index("band")
    y, z = lax.rem(group, 4), group // 4
    right_z, left_z = lax.rem(z + 1, 4) * 4 + y, lax.rem(z + 3, 4) * 4 + y

    loads = [
        pltpu.make_async_copy(own_hbm, own, load_sem.at[0]),
        pltpu.make_async_copy(left_hbm, table_l, load_sem.at[1]),
        pltpu.make_async_copy(right_hbm, table_r, load_sem.at[2]),
        pltpu.make_async_copy(kernel_hbm, weight.at[pl.ds(0, 4 * N)], load_sem.at[3]),
    ]
    for load in loads:
        load.start()

    barrier = pltpu.get_barrier_semaphore()

    def mate(k):
        return z * 4 + lax.rem(y + k, 4)

    for k in range(1, 4):
        pl.semaphore_signal(barrier, inc=1, device_id={"band": mate(k)}, device_id_type=MESH)
    for other in (right_z, left_z):
        pl.semaphore_signal(barrier, inc=1, device_id={"band": other}, device_id_type=MESH)

    def greet(i, carry):
        pl.semaphore_signal(
            barrier, inc=1, device_id={"fft": lax.rem(me + i, FFT)}, device_id_type=MESH
        )
        return carry

    lax.fori_loop(1, FFT, greet, 0)
    pl.semaphore_wait(barrier, 5 + FFT - 1)

    def rows(half):
        return pl.ds(half * (N // 2), N // 2)

    def piece(p, half):
        return block.at[p, y, rows(half)]

    def pass_on(p, half, way):
        there = right_z if way == RIGHT else left_z
        return pltpu.make_async_remote_copy(
            piece(p, half), piece(p, half),
            ring_send.at[p, half, way], ring_recv.at[p, half],
            device_id={"band": there}, device_id_type=MESH,
        )

    def share(p, half):
        for k in range(1, 4):
            pltpu.make_async_remote_copy(
                piece(p, half), piece(p, half),
                mate_send, mate_recv.at[p],
                device_id={"band": mate(k)}, device_id_type=MESH,
            ).start()

    def spread(p):
        for k in range(1, 4):
            there = lax.rem(y + k, 4)
            pltpu.make_async_remote_copy(
                own_hbm.at[p, there], cand.at[p, y],
                cand_send, cand_recv.at[p],
                device_id={"band": mate(k)}, device_id_type=MESH,
            ).start()

    place = lax.rem(z - root_z + 4, 4)

    @pl.when(place == 0)
    def _():
        eager = root_z == 0
        for p in range(4 if eager else 2):
            spread(p)
        loads[0].wait()
        root_y = lax.rem(owner_ref[0], 4)
        for p in range(4):
            cand[p, y] = own[p, y]
        for p in range(4):
            three = cand.at[p, pl.ds(0, 3)]
            pltpu.make_async_copy(three, three, cand_recv.at[p]).wait()
            if p < 2 and not eager:
                spread(p + 2)
            chosen = cand[p, 0]
            for k in range(1, 4):
                chosen = jnp.where(root_y == k, cand[p, k], chosen)
            block[p, y] = chosen
            for half, way in routes[root_z]:
                if p >= DEPTH:
                    pass_on(p - DEPTH, half, way).wait_send()
                pass_on(p, half, way).start()
            if eager:
                share(p, 0)
                share(p, 1)
        for p in () if eager else range(4):
            share(p, 0)
            share(p, 1)
        three = cand.at[:, pl.ds(0, 3)]
        pltpu.make_async_copy(three, three, cand_send).wait()

    def relay(here):
        order = [(steps[here][half] * STEP + p, p, half) for p in range(4) for half in range(2)]
        for _, p, half in sorted(order):
            pltpu.make_async_copy(piece(p, half), piece(p, half), ring_recv.at[p, half]).wait()
            for which, way in routes[here]:
                if which == half:
                    pass_on(p, half, way).start()
            share(p, half)

    for here in range(4):
        if here != root_z:
            pl.when(z == here)(functools.partial(relay, here))

    @pl.when(place != 0)
    def _():
        loads[0].wait()

    for load in loads[1:]:
        load.wait()

    def own_band(p):
        band = jnp.int32(0)
        for j in range(1, 4):
            band = jnp.where(pair_ref[0, j] == p, j, band)
        return band

    def ship(step, f):
        pltpu.make_async_copy(
            send.at[step, f, me], recv.at[step, f, me], own_sem.at[step, f]
        ).start()

        def one(i, carry):
            there = lax.rem(me + i, FFT)
            pltpu.make_async_remote_copy(
                send.at[step, f, there], recv.at[step, f, me],
                data_send.at[step, f], data_recv.at[step, f],
                device_id={"fft": there}, device_id_type=MESH,
            ).start()
            pltpu.make_async_remote_copy(
                scale_out.at[step, f], scale_in.at[step, f, me],
                scale_send.at[step, f], scale_recv.at[step, f],
                device_id={"fft": there}, device_id_type=MESH,
            ).start()
            return carry

        lax.fori_loop(1, FFT, one, 0)

    def landed(step, f):
        most = pl.ds(0, FFT - 1)
        for buffer, sem in ((recv, data_recv), (scale_in, scale_recv)):
            here = buffer.at[step, f, most]
            pltpu.make_async_copy(here, here, sem.at[step, f]).wait()
        here = recv.at[step, f, 0]
        pltpu.make_async_copy(here, here, own_sem.at[step, f]).wait()

    def encode(step, f, pieces):
        top = jnp.max(jnp.abs(pieces[0]), axis=0, keepdims=True)
        for piece in pieces[1:]:
            top = jnp.maximum(top, jnp.max(jnp.abs(piece), axis=0, keepdims=True))
        top = jnp.maximum(jnp.max(top, axis=1, keepdims=True), 1e-36)
        inverse_scale = 1.0 / top
        scale = jnp.broadcast_to(top * (1.0 / (TOP * TOP)), (1, N))
        scale_out[step, f] = scale
        scale_in[step, f, me] = scale
        for pair in range(2):
            both = jnp.concatenate(
                [pieces[2 * pair].reshape(FFT, 8, N), pieces[2 * pair + 1].reshape(FFT, 8, N)],
                axis=1,
            )
            send[step, f, :, pair] = code(both, inverse_scale)

    def decode(step, f):
        raw = recv[step, f].astype(jnp.int32).astype(jnp.float32)
        value = raw * jnp.abs(raw) * scale_in[step, f].reshape(FFT, 1, 1, N)
        decoded[pl.ds(0, FFT * 32), :] = value.reshape(FFT * 32, N)

    def line(row):
        return decoded[pl.ds(row, N, stride=8), :]

    def put(row, column, value):
        high, low = split(value)
        at = pl.ds(column, value.shape[1])
        rhs[pl.ds(row, N), at] = high
        rhs[pl.ds(row + 2 * N, N), at] = low
        rhs[pl.ds(row + 4 * N, N), at] = high

    def forward(f):
        for p in (2 * f, 2 * f + 1):
            others = block.at[p, pl.ds(0, 3)]
            pltpu.make_async_copy(others, others, mate_recv.at[p]).wait()
        densities = []
        for p in (2 * f, 2 * f + 1):
            density = block[p].astype(jnp.float32) * own[own_band(p)].astype(jnp.float32)
            densities.append(split(density.reshape(4 * N, N)))
        (high_0, low_0), (high_1, low_1) = densities
        lhs = jnp.concatenate([high_0, high_1, low_0, low_1, high_0, high_1], axis=1)
        mid[...] = dot(lhs, table_r[0])
        pieces = []
        for pair in range(2):
            for second in range(2):
                for part in range(2):
                    at = pl.ds((2 * pair + second) * N, N)
                    put(part * N, second * N, mid[at, pl.ds(part * N, N)])
            result = dot(table_l[0], rhs[:, pl.ds(0, 2 * N)])
            pieces += [result[:, :N], result[:, N:]]
        encode(0, f, pieces)
        ship(0, f)

    def middle(f):
        landed(0, f)
        decode(0, f)
        for part in range(2):
            for r in range(4):
                put(part * N, r * N, line(part * 4 + r))
        spectrum = dot(table_l[1], rhs[...])
        for r in range(4):
            factor = weight[pl.ds(r, N, stride=4), :]
            for part in range(2):
                put(part * N, r * N, spectrum[part * N : (part + 1) * N, r * N : (r + 1) * N] * factor)
        result = dot(table_l[2], rhs[...])
        encode(1, f, [result[:, r * N : (r + 1) * N] for r in range(4)])
        ship(1, f)

    def backward(f):
        landed(1, f)
        decode(1, f)
        for pair in range(2):
            for second in range(2):
                for part in range(2):
                    put(part * N, second * N, line((2 * pair + second) * 2 + part))
            field = dot(table_l[3], rhs[:, pl.ds(0, 2 * N)])
            lhs = []
            for second in range(2):
                at = slice(second * N, (second + 1) * N)
                high_0, low_0 = split(field[:N, at])
                high_1, low_1 = split(field[N:, at])
                lhs.append(jnp.concatenate([high_0, high_1, low_0, low_1, high_0, high_1], axis=1))
            potential = dot(jnp.concatenate(lhs, axis=0), table_r[1])
            for part in range(2):
                p = 2 * f + part
                at = pl.ds(2 * pair, 2)
                partner = block[p, at].astype(jnp.float32)
                product[p, at] = -(partner * potential[:, part * N : (part + 1) * N].reshape(2, N, N))

    forward(0)
    forward(1)
    middle(0)
    middle(1)
    backward(0)
    backward(1)

    for j in range(4):
        out_ref[j] = product[pair_ref[0, j]]

    def sent(here):
        for p in range(4 - DEPTH if here == root_z else 0, 4):
            for half, way in routes[here]:
                pass_on(p, half, way).wait_send()

    for here in range(4):
        if routes[here]:
            pl.when(z == here)(functools.partial(sent, here))

    here = block.at[:, pl.ds(0, 3)]
    pltpu.make_async_copy(here, here, mate_send).wait()
    for step in range(2):
        for f in range(2):
            here = send.at[step, f, pl.ds(0, FFT - 1)]
            pltpu.make_async_copy(here, here, data_send.at[step, f]).wait()
            here = scale_in.at[step, f, pl.ds(0, FFT - 1)]
            pltpu.make_async_copy(here, here, scale_send.at[step, f]).wait()


def call(root_z, owner, pairing, orbitals, kernel, lefts, rights):
    anywhere = pl.BlockSpec(memory_space=pl.ANY)
    scalars = pl.BlockSpec(memory_space=pltpu.SMEM)
    dma = pltpu.SemaphoreType.DMA
    return pl.pallas_call(
        functools.partial(exchange_kernel, root_z),
        out_shape=jax.ShapeDtypeStruct((4, 4, N, N), jnp.float32),
        in_specs=[scalars, scalars, anywhere, anywhere, anywhere, anywhere],
        out_specs=pl.BlockSpec(memory_space=pltpu.VMEM),
        scratch_shapes=[
            pltpu.VMEM((4, 4, N, N), jnp.bfloat16),
            pltpu.VMEM((4, 2 * N, 6 * N), jnp.bfloat16),
            pltpu.VMEM((2, 6 * N, 2 * N), jnp.bfloat16),
            pltpu.VMEM((4 * N + 8, N), jnp.float32),
            pltpu.VMEM((4, 4, N, N), jnp.bfloat16),
            pltpu.VMEM((4, 4, N, N), jnp.bfloat16),
            pltpu.VMEM((2, 2, FFT, 2, 16, N), jnp.int16),
            pltpu.VMEM((2, 2, FFT, 2, 16, N), jnp.int16),
            pltpu.VMEM((2, 2, 1, N), jnp.float32),
            pltpu.VMEM((2, 2, FFT, 1, N), jnp.float32),
            pltpu.VMEM((FFT * 32 + 8, N), jnp.float32),
            pltpu.VMEM((6 * N, 4 * N), jnp.bfloat16),
            pltpu.VMEM((4 * N, 2 * N), jnp.float32),
            pltpu.VMEM((4, 4, N, N), jnp.float32),
            dma((4,)),
            dma,
            dma((4,)),
            dma((4, 2, 2)),
            dma((4, 2)),
            dma,
            dma((4,)),
            dma((2, 2)),
            dma((2, 2)),
            dma((2, 2)),
            dma((2, 2)),
            dma((2, 2)),
        ],
        compiler_params=pltpu.CompilerParams(
            collective_id=root_z, has_side_effects=True, vmem_limit_bytes=48 * 1024 * 1024
        ),
    )(owner, pairing, orbitals, kernel, lefts, rights)


def local(orbitals, kernel, pairing, owner):
    lefts, rights = tables()
    root_z = (owner[0] % 16) // 4
    return lax.switch(
        root_z,
        [functools.partial(call, k) for k in range(4)],
        owner, pairing, orbitals, kernel.reshape(4 * N, N), jnp.asarray(lefts), jnp.asarray(rights),
    )


def solution(mesh):
    placed = (P("band", "fft", None, None), P(None, "fft", None), P("band", None), P())
    return jax.shard_map(
        local, mesh=mesh, in_specs=placed, out_specs=P("band", "fft", None, None), check_vma=False
    )
```
